256 devices in a mesh: seq: 16 (over y, x), exp: 16 (over z, core).
Axes of the slice: x: 4, y: 4, z: 8, core: 2. Of those that a mesh axis runs over, the one named last changes fastest.
Arguments:
- residual: bfloat16 [16, 2048, 2048], P('exp', 'seq'), may hold values from -6 to 6
- query_nope: bfloat16 [16, 2048, 1024], P('exp', 'seq'), may hold values from -6 to 6
- query_rope: bfloat16 [16, 2048, 512], P('exp', 'seq'), may hold values from -16 to 16
- latent_rows: bfloat16 [16, 2048, 512], P('exp', 'seq'), may hold values from -6 to 6
- key_rope: bfloat16 [16, 2048, 64], P('exp', 'seq'), may hold values from -6 to 6
- key_up: bfloat16 [512, 1024], replicated, may hold values from -0.25 to 0.25
- value_up: bfloat16 [512, 1024], replicated, may hold values from -0.25 to 0.25
- output_proj: bfloat16 [1024, 2048], replicated, may hold values from -0.1875 to 0.1875
- doc_lengths: int32 [16, 8], P('exp'), may hold values from 1 to 384, 2048 in all within a row
- norm_gain: bfloat16 [2048], replicated, may hold values from 0.099609375 to 1.8984375
- router_weight: bfloat16 [2048, 64], replicated, may hold values from -0.125 to 0.125
- expert_ids: int32 [16, 2048, 6], P('exp', 'seq'), may hold values from 0 to 63, all different within a row; in each aligned block of 128 rows (0 to 127, 128 to 255, ..., all dimensions but the last counted through in order) at most 12 rows name the same one
- gate_quarter: bfloat16 [16, 16, 2048, 352], P('seq', 'exp'), may hold values from -0.125 to 0.125
- up_quarter: bfloat16 [16, 16, 2048, 352], P('seq', 'exp'), may hold values from -0.125 to 0.125
- down_quarter: bfloat16 [16, 16, 352, 2048], P('seq', 'exp'), may hold values from -0.15625 to 0.15625
Outputs:
- mixed: bfloat16 [16, 2048, 2048], P('exp', 'seq')
The draws below stay inside these ranges and needn't reach their ends.
Inputs may be any that keep to these rules, and one draw needn't show every extreme that they name: `doc_lengths`: the longest document of each pack has exactly 384 tokens. `expert_ids`: each token names 6 different experts; the rows of one device name every expert exactly 12 times.
All inputs are finite; a program needn't handle non-finite values.
Results may differ from the reference program's by a relative error of at most 0.01.
Values may be sent and summed in bfloat16 or wider, within the bound.
A program may use at most 128 MiB of HBM per device.

```python
import math
import jax
import jax.numpy as jnp
import numpy as np
from jax import lax

D = 2048
HEADS = 8
NOPE = 128
ROPE = 64
VDIM = 128
LATENT = 512
FF = 1408
TOP = 6
KS = 3
TOK_DEV = 128
PACKS = 16
PLEN = 2048
EXPERTS = 64
FQ = 352
MOST = 12
MAXDOC = 384
NDOCS = 8
N_SEQ = 16
N_EXP = 16


def draw_key_rope(key, part):
    key = jax.random.fold_in(key, 3)
    own_noise = jnp.clip(jax.random.normal(key, (PACKS, PLEN, ROPE), jnp.float32), -6.0, 6.0)
    return own_noise.astype(jnp.bfloat16)


def draw_query_rope(key, part):
    key = jax.random.fold_in(key, 5)
    own_noise = jnp.clip(jax.random.normal(key, (PACKS, PLEN, HEADS, ROPE), jnp.float32), -6.0, 6.0)
    return own_noise.reshape(PACKS, PLEN, HEADS * ROPE).astype(jnp.bfloat16)


def steps_of(stream_key, extent, shards, low, high):
    gain = 1.0
    for dim, blocks in shards:
        steps = jax.random.uniform(jax.random.fold_in(jax.random.fold_in(stream_key, 6), dim), (blocks,), jnp.float32, low / len(shards), high / len(shards))
        gain = gain * jnp.repeat(jnp.exp(steps), extent[dim] // blocks).reshape((-1,) + (1,) * (len(extent) - 1 - dim))
    return gain


def length_profile(count, total, limit, slope):
    weights = [(1 << 20) // math.isqrt(standing ** slope) + 1 for standing in range(2, count + 1)]
    rest, counts = total - limit - (count - 1), [1] * (count - 1)
    while rest > 0:
        free = [i for i in range(count - 1) if counts[i] < limit]
        mass, budget = sum([weights[i] for i in free]), rest
        for i in free:
            more = min(limit - counts[i], max(1, budget * weights[i] // mass), rest)
            counts[i] = counts[i] + more
            rest = rest - more
    return np.array([limit] + counts)


def ragged(own_key, number_of, total, most, slope):
    if number_of == 2:
        one = jax.random.randint(own_key, (), max(1, total - most), min(most, total - 1) + 1)
        return jnp.stack([one, total - one])
    tallies = jnp.asarray(length_profile(number_of, total, most, slope), jnp.int32)
    couples = (number_of - 1) // 2
    source_of, receiver = tallies[1:1 + 2 * couples:2], tallies[2:2 + 2 * couples:2]
    slack = jnp.minimum(source_of - 1, most - receiver)
    moved = jax.random.randint(jax.random.fold_in(own_key, 1), (couples,), 0, 1 << 20) % (slack + 1)
    tallies = tallies.at[1:1 + 2 * couples:2].set(source_of - moved).at[2:2 + 2 * couples:2].set(receiver + moved)
    return tallies[jax.random.permutation(jax.random.fold_in(own_key, 2), number_of)]


def assign_block(rng, own, number, rows, amount, top, bound, skew):
    ranking = jax.random.permutation(rng, amount)
    heavy_load, ordinary = portions_of(amount, rows * top, bound, skew, True), portions_of(amount, rows * top, bound, skew, False)
    places = jnp.arange(amount)

    def named(sizes, offset_by):
        used = int((sizes > 0).sum())
        fixed = max(1, used // 4)
        moved = fixed + (places - fixed + offset_by * (used - fixed)) % max(1, amount - fixed)
        return jnp.zeros((amount,), jnp.int32).at[ranking[jnp.where(places < fixed, places, moved)]].set(jnp.asarray(sizes, jnp.int32))

    sizes = jnp.where(number % 4 == 0, named(heavy_load, number // 4), named(ordinary, number - number // 4 - 1))
    mixed = jax.random.permutation(jax.random.fold_in(own, 3), amount)
    giver, taker = mixed[0:amount // 2 * 2:2], mixed[1:amount // 2 * 2:2]
    room = jnp.minimum(sizes[giver] - 1, bound - sizes[taker]) // 2
    room = jnp.where((giver == ranking[0]) | (taker == ranking[0]) | (sizes[taker] == 0), 0, jnp.maximum(room, 0))
    moved = jax.random.randint(jax.random.fold_in(own, 4), (amount // 2,), 0, 1 << 20) % (room + 1)
    sizes = sizes.at[giver].add(-moved).at[taker].add(moved)
    items = jnp.searchsorted(jnp.cumsum(sizes), jnp.arange(rows * top), side="right").astype(jnp.int32)
    table = items.reshape(top, rows).T
    table = table[jax.random.permutation(jax.random.fold_in(own, 1), rows)]
    offset_by = jax.random.randint(jax.random.fold_in(own, 2), (rows, 1), 0, top)
    return jnp.take_along_axis(table, (jnp.arange(top)[None, :] + offset_by) % top, axis=1)


def portions_of(amount, total, reach, lean, full):
    weights = [(1 << 20) // math.isqrt(standing ** lean) + 1 for standing in range(1, amount + 1)]
    largest = reach if full else min(reach, max(-(-total // amount), total * weights[0] // sum(weights)))
    least = 1 if total - largest >= amount - 1 else 0
    counts, rest = [largest] + [least] * (amount - 1), total - largest - least * (amount - 1)
    while rest > 0:
        movable = [i for i in range(1, amount) if counts[i] < largest] or [i for i in range(1, amount) if counts[i] < reach]
        mass, remaining = sum([weights[i] for i in movable]), rest
        for i in movable:
            addition = min(reach - counts[i], max(1, remaining * weights[i] // mass), rest)
            counts[i] = counts[i] + addition
            rest = rest - addition
    return np.array(counts)


def centred(own_key, shape, spread, most, split=(), kind=jnp.bfloat16):
    result = jax.random.normal(own_key, shape, jnp.float32) * spread
    if len(split) > 0:
        result = steps_of(own_key, shape, split, -0.22, 0.18) * result
    return jnp.clip(result, min=-most, max=most).astype(kind)


def setup_inputs(seed: int = 0) -> dict:
    arg_keys = jax.random.split(jax.random.key(seed), 16)
    residual = centred(arg_keys[0], (PACKS, PLEN, D), 1.0, 6.0, ((0, 16), (1, 16)))
    query_nope = centred(arg_keys[1], (PACKS, PLEN, HEADS * NOPE), 1.0, 6.0, ((0, 16), (1, 16)))
    query_rope = draw_query_rope(jax.random.fold_in(arg_keys[15], 71), 0)
    latent_rows = centred(arg_keys[3], (PACKS, PLEN, LATENT), 1.0, 6.0, ((0, 16), (1, 16)))
    key_rope = draw_key_rope(jax.random.fold_in(arg_keys[15], 71), 0)
    key_up = centred(arg_keys[5], (LATENT, HEADS * NOPE), LATENT ** -0.5, 0.25)
    value_up = centred(arg_keys[6], (LATENT, HEADS * VDIM), LATENT ** -0.5, 0.25)
    output_proj = centred(arg_keys[7], (HEADS * VDIM, D), (HEADS * VDIM) ** -0.5, 0.1875)
    doc_lengths = jax.vmap(lambda own: ragged(own, NDOCS, PLEN, MAXDOC, 2))(jax.random.split(arg_keys[8], PACKS)).reshape((PACKS, NDOCS)).astype(jnp.int32)
    norm_gain = jnp.clip(1.0 + 0.18 * jax.random.normal(arg_keys[9], (D,), jnp.float32), 0.099609375, 1.8984375).astype(jnp.bfloat16)
    router_weight = centred(arg_keys[10], (D, EXPERTS), D ** -0.5, 0.125)
    expert_ids_keys = jax.random.split(jax.random.fold_in(arg_keys[11], 1), PACKS * PLEN // TOK_DEV)
    expert_ids_turns = jax.random.permutation(jax.random.fold_in(arg_keys[11], 3), PACKS * PLEN // TOK_DEV)
    expert_ids = jax.vmap(lambda own, number: assign_block(jax.random.fold_in(arg_keys[11], 2), own, number, TOK_DEV, EXPERTS, TOP, MOST, 0))(expert_ids_keys, expert_ids_turns).reshape((PACKS, PLEN, TOP))
    gate_quarter = centred(arg_keys[12], (N_SEQ, N_EXP, D, FQ), D ** -0.5, 0.125, ((0, 16), (1, 16)))
    up_quarter = centred(arg_keys[13], (N_SEQ, N_EXP, D, FQ), D ** -0.5, 0.125, ((0, 16), (1, 16)))
    down_quarter = centred(arg_keys[14], (N_SEQ, N_EXP, FQ, D), FF ** -0.5, 0.15625, ((0, 16), (1, 16)))
    return dict(residual=residual, query_nope=query_nope, query_rope=query_rope, latent_rows=latent_rows, key_rope=key_rope, key_up=key_up, value_up=value_up, output_proj=output_proj, doc_lengths=doc_lengths, norm_gain=norm_gain, router_weight=router_weight, expert_ids=expert_ids, gate_quarter=gate_quarter, up_quarter=up_quarter, down_quarter=down_quarter)


def document_of(lengths, positions):
    starts = jnp.cumsum(lengths) - lengths
    return lax.optimization_barrier(jnp.sum((positions[:, None] >= starts[None, :]).astype(jnp.int32), axis=1)) - 1

def reference(residual, query_nope, query_rope, latent_rows, key_rope, key_up, value_up, output_proj, doc_lengths, norm_gain, router_weight, expert_ids, gate_quarter, up_quarter, down_quarter):
    window = KS * TOK_DEV
    span = window + TOK_DEV
    score_scale = 1.0 / math.sqrt(NOPE + ROPE)
    block_total = PLEN // TOK_DEV

    def one_pack(pack_index):
        lengths = doc_lengths[pack_index]
        key_rows = jnp.dot(latent_rows[pack_index], key_up, preferred_element_type=jnp.float32).astype(jnp.bfloat16)
        value_rows = jnp.dot(latent_rows[pack_index], value_up, preferred_element_type=jnp.float32).astype(jnp.bfloat16)
        positions = jnp.arange(PLEN, dtype=jnp.int32)
        documents = document_of(lengths, positions)
        key_padded = jnp.concatenate([jnp.zeros((window, HEADS * NOPE), jnp.bfloat16), key_rows], 0)
        value_padded = jnp.concatenate([jnp.zeros((window, HEADS * VDIM), jnp.bfloat16), value_rows], 0)
        rope_padded = jnp.concatenate([jnp.zeros((window, ROPE), jnp.bfloat16), key_rope[pack_index]], 0)
        docs_padded = jnp.concatenate([jnp.full((window,), -1, jnp.int32), documents], 0)
        where_padded = jnp.concatenate([jnp.arange(window, dtype=jnp.int32) - window, positions], 0)

        def one_block(block_index):
            begin_at = block_index * TOK_DEV
            query_one = lax.dynamic_slice_in_dim(query_nope[pack_index], begin_at, TOK_DEV, 0).reshape(TOK_DEV, HEADS, NOPE).astype(jnp.float32)
            query_two = lax.dynamic_slice_in_dim(query_rope[pack_index], begin_at, TOK_DEV, 0).reshape(TOK_DEV, HEADS, ROPE).astype(jnp.float32)
            query_docs = lax.dynamic_slice_in_dim(documents, begin_at, TOK_DEV, 0)
            query_where = lax.dynamic_slice_in_dim(positions, begin_at, TOK_DEV, 0)
            key_one = lax.dynamic_slice_in_dim(key_padded, begin_at, span, 0).reshape(span, HEADS, NOPE).astype(jnp.float32)
            key_two = lax.dynamic_slice_in_dim(rope_padded, begin_at, span, 0).astype(jnp.float32)
            value_one = lax.dynamic_slice_in_dim(value_padded, begin_at, span, 0).reshape(span, HEADS, VDIM).astype(jnp.float32)
            key_docs = lax.dynamic_slice_in_dim(docs_padded, begin_at, span, 0)
            key_where = lax.dynamic_slice_in_dim(where_padded, begin_at, span, 0)
            scores = (jnp.einsum('qhd,khd->hqk', query_one, key_one) + jnp.einsum('qhd,kd->hqk', query_two, key_two)) * score_scale
            allowed = (query_docs[:, None] == key_docs[None, :]) & (key_where[None, :] <= query_where[:, None]) & (key_docs[None, :] >= 0)
            row_max = lax.optimization_barrier(jnp.max(jnp.where(allowed[None], scores, -jnp.inf), axis=2, keepdims=True))
            weights = jnp.where(allowed[None], jnp.exp(scores - row_max), 0.0)
            totals = lax.optimization_barrier(jnp.sum(weights, axis=2))
            rounded = lax.optimization_barrier(weights.astype(jnp.bfloat16)).astype(jnp.float32)
            head_rows = jnp.einsum('hqk,khd->qhd', rounded, value_one) / totals.T[:, :, None]
            return head_rows.reshape(TOK_DEV, HEADS * VDIM).astype(jnp.bfloat16)
        head_out = lax.map(one_block, jnp.arange(block_total, dtype=jnp.int32)).reshape(PLEN, HEADS * VDIM)
        return jnp.dot(head_out, output_proj, preferred_element_type=jnp.float32)
    attention = lax.map(one_pack, jnp.arange(PACKS, dtype=jnp.int32))
    token_total = PACKS * PLEN
    flattened = (residual.astype(jnp.float32) + attention).reshape(token_total, D)
    normed = (flattened * lax.rsqrt(lax.optimization_barrier(jnp.mean(flattened * flattened, axis=1, keepdims=True)) + 1e-06) * norm_gain.astype(jnp.float32)).astype(jnp.bfloat16)
    logits = jnp.dot(normed, router_weight, preferred_element_type=jnp.float32)
    choice_ids = expert_ids.reshape(token_total, TOP)
    chosen = jnp.take_along_axis(jax.nn.sigmoid(logits), choice_ids, axis=1)
    gate_values = chosen / lax.optimization_barrier(jnp.sum(chosen, axis=1, keepdims=True)) * 2.446
    choice_flat = choice_ids.reshape(-1)
    gate_flat = gate_values.reshape(-1)
    per_expert = token_total * TOP // EXPERTS

    def one_expert(accum, expert):
        picked = jnp.nonzero(choice_flat == expert, size=per_expert)[0].astype(jnp.int32)
        token_index = picked // TOP
        rows_in = normed[token_index]
        expert_group = expert // N_EXP
        column = expert % N_EXP
        anchor = jnp.zeros((), jnp.int32)
        start_at = (4 * expert_group, column, anchor, anchor)
        gate_full = lax.dynamic_slice(gate_quarter, start_at, (4, 1, D, FQ)).reshape(4, D, FQ).transpose(1, 0, 2).reshape(D, FF)
        up_full = lax.dynamic_slice(up_quarter, start_at, (4, 1, D, FQ)).reshape(4, D, FQ).transpose(1, 0, 2).reshape(D, FF)
        down_full = lax.dynamic_slice(down_quarter, start_at, (4, 1, FQ, D)).reshape(FF, D)
        activation = jax.nn.silu(jnp.dot(rows_in, gate_full, preferred_element_type=jnp.float32)) * jnp.dot(rows_in, up_full, preferred_element_type=jnp.float32)
        hidden_units = activation.astype(jnp.bfloat16)
        expert_out = jnp.dot(hidden_units, down_full, preferred_element_type=jnp.float32).astype(jnp.bfloat16)
        contrib = expert_out.astype(jnp.float32) * gate_flat[picked][:, None]
        return (accum.at[token_index].add(contrib), None)
    routed, unused = lax.scan(one_expert, jnp.zeros((token_total, D), jnp.float32), jnp.arange(EXPERTS, dtype=jnp.int32))
    return (flattened + routed).astype(jnp.bfloat16).reshape(PACKS, PLEN, D)
```

```python
import functools
import math

import jax
import jax.numpy as jnp
from jax import lax
from jax.experimental import pallas as pl
from jax.experimental.pallas import tpu as pltpu
from jax.sharding import PartitionSpec as P

MESH = pl.DeviceIdType.MESH
F32 = jnp.float32
BF16 = jnp.bfloat16

D = 2048
HEADS = 8
NOPE = 128
ROPE = 64
LATENT = 512
TOP = 6
KS = 3
T = 128
EXPERTS = 64
FQ = 352
SLOTS = 12
NX, NY, NZ = 4, 4, 8
BLOCK = NZ * SLOTS
WORK = 2 * NY * BLOCK
EXTRA = 128
NC = 4
CW = D // NC
NJ = 4
JW = D // NJ


def dot(a, b):
    return jnp.dot(a, b, preferred_element_type=F32)


def dot_t(a, b):
    return lax.dot_general(a, b, (((1,), (1,)), ((), ())), preferred_element_type=F32)


def iota(shape, dim):
    return lax.broadcasted_iota(jnp.int32, shape, dim).astype(F32)


def lanes_of(c):
    if c == 0:
        return pl.ds(0, EXTRA + CW)
    return pl.ds(EXTRA + c * CW, CW)


def kernel(
    residual,
    query_nope,
    query_rope,
    latent,
    rope,
    lengths,
    gain,
    router,
    ids,
    key_up_in,
    value_up_in,
    proj_in,
    gate_in,
    up_in,
    down_in,
    out,
    key_up,
    value_up,
    proj,
    w_gate,
    w_up,
    w_down,
    latents,
    keys,
    values,
    head_out,
    hidden,
    tok,
    code_rows,
    code_cols,
    pick,
    put,
    outbox,
    work,
    units,
    inbox,
    zs,
    zr,
    load_sem,
    a_send,
    a_recv,
    w_send,
    w_recv,
    f_send,
    f_recv,
    d_send,
    d_recv,
    e_send,
    e_recv,
    z_send,
    z_recv,
    y_send,
    y_recv,
    r_send,
    r_recv,
    s_send,
    s_recv,
):
    seq = lax.axis_index("seq")
    exp = lax.axis_index("exp")
    my_y, my_x = lax.div(seq, NX), lax.rem(seq, NX)
    my_z, my_c = lax.div(exp, 2), lax.rem(exp, 2)

    def peer(dx=0, dy=0, dz=0, dc=0):
        x = lax.rem(my_x + (dx + NX), NX)
        y = lax.rem(my_y + (dy + NY), NY)
        z = lax.rem(my_z + (dz + NZ), NZ)
        c = lax.rem(my_c + dc, 2)
        return (y * NX + x, z * 2 + c)

    def later(distance):
        return (lax.rem(seq + (distance + NX * NY), NX * NY), exp)

    def send(src, dst, send_sem, recv_sem, device):
        copy = pltpu.make_async_remote_copy(
            src_ref=src,
            dst_ref=dst,
            send_sem=send_sem,
            recv_sem=recv_sem,
            device_id=device,
            device_id_type=MESH,
        )
        copy.start()
        return copy

    started = []

    loads = []
    for i, (src, dst) in enumerate(
        (
            (key_up_in, key_up),
            (value_up_in, value_up),
            (proj_in, proj),
            (gate_in.at[0, 0], w_gate.at[0]),
            (up_in.at[0, 0], w_up.at[0]),
            (down_in.at[0, 0], w_down.at[0]),
        )
    ):
        copy = pltpu.make_async_copy(src, dst, load_sem.at[i])
        copy.start()
        loads.append(copy)

    partners = [later(d) for d in (1, 2, 3, -1, -2, -3)]
    partners += [peer(dx=1), peer(dx=-1), peer(dz=1), peer(dz=-1)]
    partners += [peer(dy=b // 2, dc=b % 2) for b in range(1, 2 * NY)]
    barrier = pltpu.get_barrier_semaphore()
    for device in partners:
        pl.semaphore_signal(barrier, inc=1, device_id=device, device_id_type=MESH)

    twice = (
        lax.rem(lax.broadcasted_iota(jnp.int32, (ROPE, 2 * ROPE), 1), ROPE)
        == lax.broadcasted_iota(jnp.int32, (ROPE, 2 * ROPE), 0)
    ).astype(F32).astype(BF16)
    latents[0, :, :LATENT] = latent[0]
    latents[0, :, LATENT:] = dot(rope[0], twice).astype(BF16)

    pl.semaphore_wait(barrier, len(partners))

    arriving = []
    for d in (1, 2, 3):
        copy = send(latents.at[0], latents.at[d], a_send.at[d - 1], a_recv.at[d - 1], later(d))
        arriving.append(copy)
        started.append(copy)

    near = []
    for i, (src, dst) in enumerate(((gate_in, w_gate), (up_in, w_up))):
        for way, dx in ((0, 1), (1, -1)):
            copy = send(
                src.at[0, 0], dst.at[1 + way], w_send.at[i, way], w_recv.at[i, way], peer(dx=dx)
            )
            near.append(copy)
            started.append(copy)

    lane_e = iota((T, EXPERTS), 1)
    id_cols = ids[0].astype(F32)
    hits = [(id_cols[:, j : j + 1] == lane_e).astype(F32) for j in range(TOP)]
    named = functools.reduce(jnp.add, hits)
    lower = (
        lax.broadcasted_iota(jnp.int32, (T, T), 0) >= lax.broadcasted_iota(jnp.int32, (T, T), 1)
    ).astype(F32).astype(BF16)
    counted = dot(lower, named.astype(BF16))
    ranks = [jnp.sum(hit * counted, axis=1, keepdims=True) - 1.0 for hit in hits]

    def codes(shape, dim):
        row = iota(shape, dim)
        block = jnp.floor((row + 0.5) * (1.0 / BLOCK))
        rest = row - block * BLOCK
        source = jnp.floor((rest + 0.5) * (1.0 / SLOTS))
        rank = rest - source * SLOTS
        dy = jnp.floor((block + 0.5) * 0.5)
        dc = block - dy * 2.0
        y = dy + my_y.astype(F32)
        y = jnp.where(y >= NY, y - NY, y)
        c = dc + my_c.astype(F32)
        c = jnp.where(c >= 2.0, c - 2.0, c)
        expert = y * 16.0 + my_z.astype(F32) * 2.0 + c
        return source * 1024.0 + expert * 16.0 + rank

    code_rows[...] = codes((WORK, T), 0)
    code_cols[...] = codes((8, WORK), 1)

    loads[0].wait()
    loads[1].wait()

    def project(d):
        rows = pl.ds(pl.multiple_of(d * T, T), T)
        block = latents[d, :, :LATENT]
        keys[rows, :] = dot(block, key_up[...]).astype(BF16)
        values[rows, :] = dot(block, value_up[...]).astype(BF16)

    project(0)
    for copy in arriving:
        copy.wait_recv()

    def project_step(d, carry):
        project(d)
        return carry

    lax.fori_loop(1, KS + 1, project_step, 0)

    span = (KS + 1) * T
    first = seq * T
    query_where = first + lax.broadcasted_iota(jnp.int32, (T, 1), 0)
    col = lax.broadcasted_iota(jnp.int32, (1, span), 1)
    key_where = first + lax.rem(col, T) - lax.div(col, T) * T
    query_doc = jnp.zeros((T, 1), jnp.int32)
    key_doc = jnp.zeros((1, span), jnp.int32)
    start = jnp.int32(0)
    for n in range(lengths.shape[1]):
        query_doc += (query_where >= start).astype(jnp.int32)
        key_doc += (key_where >= start).astype(jnp.int32)
        start = start + lengths[0, n]
    allowed = (query_doc == key_doc) & (key_where <= query_where) & (key_where >= 0)
    bias = jnp.where(allowed, 0.0, -1e30)
    scale = 1.0 / math.sqrt(NOPE + ROPE)
    half = lax.broadcasted_iota(jnp.int32, (T, 2 * ROPE), 1) < ROPE

    def head_pair(pair, carry):
        pair_lanes = pl.ds(pl.multiple_of(pair * 128, 128), 128)
        q_pair = query_rope[0, :, pair_lanes]
        for odd in range(2):
            lanes = pl.ds(pl.multiple_of((pair * 2 + odd) * NOPE, 128), NOPE)
            q_two = jnp.where(half, q_pair, 0.0) if odd == 0 else jnp.where(half, 0.0, q_pair)
            q = jnp.concatenate([query_nope[0, :, lanes], q_two.astype(BF16)], axis=1)
            rope_keys = latents[:, :, LATENT:].reshape(span, 2 * ROPE)
            k = jnp.concatenate([keys[:, lanes], rope_keys], axis=1)
            scores = dot_t(q, k) * scale + bias
            weights = jnp.exp(scores - jnp.max(scores, axis=1, keepdims=True))
            totals = jnp.sum(weights, axis=1, keepdims=True)
            mixed = dot(weights.astype(BF16), values[:, lanes])
            head_out[:, lanes] = (mixed / totals).astype(BF16)
        return carry

    lax.fori_loop(0, HEADS // 2, head_pair, 0)

    loads[2].wait()

    def project_out(i, squares):
        lanes = pl.ds(pl.multiple_of(i * 512, 512), 512)
        rows = residual[0, :, lanes].astype(F32) + dot(head_out[...], proj[:, lanes])
        hidden[:, lanes] = rows
        return squares + jnp.sum(rows * rows, axis=1, keepdims=True)

    squares = lax.fori_loop(0, D // 512, project_out, jnp.zeros((T, 1), F32))
    inverse = lax.rsqrt(squares * (1.0 / D) + 1e-06)
    normed = (hidden[...] * inverse * gain[...].astype(F32)).astype(BF16)
    tok[0, :, EXTRA:] = normed
    chances = jax.nn.sigmoid(dot(normed, router[...]))
    chosen = [jnp.sum(hit * chances, axis=1, keepdims=True) for hit in hits]
    norm_by = 2.446 / functools.reduce(jnp.add, chosen)
    lane = iota((T, EXTRA), 1)
    extra = jnp.zeros((T, EXTRA), F32)
    for j in range(TOP):
        extra = jnp.where(lane == j, id_cols[:, j : j + 1], extra)
        extra = jnp.where(lane == 8 + j, ranks[j], extra)
        extra = jnp.where(lane == 16 + j, chosen[j] * norm_by, extra)
    tok[0, :, :EXTRA] = extra.astype(BF16)

    ring = {}

    def ring_send(c, hop):
        for way, dz in ((0, 1), (1, -1)):
            if hop == NZ // 2 and c % 2 != way:
                continue
            src = (hop - 1) if way == 0 else (NZ - hop + 1) % NZ
            dst = hop if way == 0 else NZ - hop
            lanes = lanes_of(c)
            copy = send(
                tok.at[src, :, lanes],
                tok.at[dst, :, lanes],
                z_send.at[way, hop - 1, c],
                z_recv.at[way, hop - 1, c],
                peer(dz=dz),
            )
            ring[c, hop, way] = copy
            started.append(copy)

    def ring_wait(c, hop):
        for way in range(2):
            if (c, hop, way) in ring:
                ring[c, hop, way].wait_recv()

    def build(s):
        x = tok[s, :, :EXTRA].astype(F32)
        source = (s * 1024).astype(F32)
        x_t = x.T
        rows = code_rows[...]
        match = None
        for j in range(TOP):
            code = x_t[j : j + 1, :] * 16.0 + x_t[8 + j : 9 + j, :] + source
            hit = rows == code
            match = hit if match is None else match | hit
        lanes = pl.ds(pl.multiple_of(s * T, T), T)
        pick[:, lanes] = match.astype(F32).astype(BF16)
        cols = code_cols[0:1, :]
        weight = jnp.zeros((T, WORK), F32)
        for j in range(TOP):
            code = x[:, j : j + 1] * 16.0 + x[:, 8 + j : 9 + j] + source
            weight = jnp.where(cols == code, x[:, 16 + j : 17 + j], weight)
        put[lanes, :] = weight.astype(BF16)

    def build_two(first_s, step, count):
        def body(i, carry):
            build(first_s + i * step)
            return carry

        lax.fori_loop(0, count, body, 0)

    handed = {}

    def hand_out(c):
        lanes = pl.ds(c * CW, CW)
        tok_lanes = pl.ds(EXTRA + c * CW, CW)

        def body(i, carry):
            rows = pl.ds(pl.multiple_of(i * (WORK // 2), WORK // 2), WORK // 2)
            block = tok[:, :, tok_lanes].reshape(NZ * T, CW)
            outbox[rows, lanes] = dot(pick[rows, :], block).astype(BF16)
            return carry

        lax.fori_loop(0, 2, body, 0)
        for b in range(1, 2 * NY):
            rows = pl.ds(b * BLOCK, BLOCK)
            copy = send(
                outbox.at[rows, lanes],
                work.at[rows, lanes],
                y_send.at[b, c],
                y_recv.at[b, c],
                peer(dy=b // 2, dc=b % 2),
            )
            handed[c, b] = copy
            started.append(copy)
        work[:BLOCK, lanes] = outbox[:BLOCK, lanes]

    far = []

    def weights_onward():
        for copy in near:
            copy.wait_recv()
        for way, (ref, dx) in enumerate(((w_gate, 1), (w_up, -1))):
            copy = send(
                ref.at[1 + way], ref.at[3], f_send.at[way], f_recv.at[way], peer(dx=dx)
            )
            far.append(copy)
            started.append(copy)
        for j in range(NJ):
            lanes = pl.ds(j * JW, JW)
            for way, dx in ((0, 1), (1, -1)):
                copy = send(
                    down_in.at[0, 0, :, lanes],
                    w_down.at[1 + way, :, lanes],
                    d_send.at[way, j],
                    d_recv.at[way, j],
                    peer(dx=dx),
                )
                down_near[j, way] = copy
                started.append(copy)

    down_near = {}
    down_far = {}

    def down_onward(j):
        lanes = pl.ds(j * JW, JW)
        for way in range(2):
            down_near[j, way].wait_recv()
        way, dx = (0, 1) if j % 2 == 0 else (1, -1)
        copy = send(
            w_down.at[1 + way, :, lanes],
            w_down.at[3, :, lanes],
            e_send.at[j],
            e_recv.at[j],
            peer(dx=dx),
        )
        down_far[j] = copy
        started.append(copy)

    ring_send(0, 1)
    ring_send(1, 1)
    build_two(0, 1, 1)
    events = sorted((2 * c + hop, c, hop) for c in range(NC) for hop in range(1, NZ // 2 + 1))
    for _, c, hop in events:
        ring_wait(c, hop)
        if hop < NZ // 2:
            ring_send(c, hop + 1)
        if hop == 2 and c + 2 < NC:
            ring_send(c + 2, 1)
        if c == 0:
            if hop < NZ // 2:
                build_two(hop, NZ - 2 * hop, 2)
            else:
                build_two(hop, 1, 1)
        if hop == NZ // 2:
            hand_out(c)
            if c == NC - 2:
                weights_onward()
    for c in range(NC):
        for b in range(1, 2 * NY):
            handed[c, b].wait_recv()

    for copy in loads[3:]:
        copy.wait()
    tile = 256

    def hidden_units(w):
        def body(i, carry):
            rows = pl.ds(pl.multiple_of(i * tile, tile), tile)
            x = work[rows, :]
            g = dot(x, w_gate[w])
            units[w, rows, :] = (g * jax.nn.sigmoid(g) * dot(x, w_up[w])).astype(BF16)
            return carry

        lax.fori_loop(0, WORK // tile, body, 0)

    for w in range(4):
        if w == 3:
            for copy in far:
                copy.wait_recv()
            down_onward(0)
        hidden_units(w)

    for copy in handed.values():
        copy.wait_send()
    back = {}

    def answer(j):
        lanes = pl.ds(j * JW, JW)
        down_far[j].wait_recv()

        def body(i, carry):
            rows = pl.ds(pl.multiple_of(i * tile, tile), tile)
            total = dot(units[0, rows, :], w_down[0, :, lanes])
            for w in range(1, 4):
                total += dot(units[w, rows, :], w_down[w, :, lanes])
            outbox[rows, lanes] = total.astype(BF16)
            return carry

        lax.fori_loop(0, WORK // tile, body, 0)
        for b in range(1, 2 * NY):
            rows = pl.ds(b * BLOCK, BLOCK)
            copy = send(
                outbox.at[rows, lanes],
                inbox.at[rows, lanes],
                r_send.at[b, j],
                r_recv.at[b, j],
                peer(dy=-(b // 2), dc=b % 2),
            )
            back[j, b] = copy
            started.append(copy)
        inbox[:BLOCK, lanes] = outbox[:BLOCK, lanes]

    sums = {}

    def sum_send(j, way, left):
        lanes = pl.ds(j * JW, JW)
        slot = left if way == 0 else NZ - left
        where = NZ // 2 * 2 - 2 if left == NZ // 2 else way * (NZ // 2 - 1) + left - 1
        copy = send(
            zs.at[slot, :, lanes],
            zr.at[where, :, lanes],
            s_send.at[way, left - 1, j],
            s_recv.at[way, left - 1, j],
            peer(dz=-1 if way == 0 else 1),
        )
        sums[j, way, left] = (copy, where)
        started.append(copy)

    def combine(j):
        lanes = pl.ds(j * JW, JW)
        for b in range(1, 2 * NY):
            back[j, b].wait_recv()

        def body(i, carry):
            rows = pl.ds(pl.multiple_of(i * 2 * T, 2 * T), 2 * T)
            total = dot(put[rows, :], inbox[:, lanes]).astype(BF16)
            zs[2 * i, :, lanes] = total[:T]
            zs[2 * i + 1, :, lanes] = total[T:]
            return carry

        lax.fori_loop(0, NZ // 2, body, 0)
        long_way = j % 2
        sum_send(j, long_way, NZ // 2)
        sum_send(j, 1 - long_way, NZ // 2 - 1)

    def reduce_step(j, hop):
        lanes = pl.ds(j * JW, JW)
        long_way = j % 2
        for way, left in ((long_way, NZ // 2 + 1 - hop), (1 - long_way, NZ // 2 - hop)):
            if left < 1:
                continue
            copy, where = sums[j, way, left]
            copy.wait_recv()
            if left > 1:
                slot = left - 1 if way == 0 else NZ - left + 1
                total = zs[slot, :, lanes].astype(F32) + zr[where, :, lanes].astype(F32)
                zs[slot, :, lanes] = total.astype(BF16)
                sum_send(j, way, left - 1)
        if hop == NZ // 2:
            total = hidden[:, lanes] + zs[0, :, lanes].astype(F32)
            for way in range(2):
                total += zr[sums[j, way, 1][1], :, lanes].astype(F32)
            out[0, :, lanes] = total.astype(BF16)

    steps = []
    for j in range(NJ):
        steps.append((3 * j, 0, j, "answer"))
        steps.append((3 * j + 3.5, 0, j, "combine"))
        for hop in range(1, NZ // 2 + 1):
            steps.append((3 * j + 4.5 + 1.1 * hop, 1, j, hop))
    for _, _, j, what in sorted(steps, key=lambda step: step[:3]):
        if what == "answer":
            if j + 1 < NJ:
                down_onward(j + 1)
            answer(j)
        elif what == "combine":
            combine(j)
        else:
            reduce_step(j, what)

    for copy in started:
        if not any(copy is other for other in handed.values()):
            copy.wait_send()


def on_device(
    residual,
    query_nope,
    query_rope,
    latent_rows,
    key_rope,
    key_up,
    value_up,
    output_proj,
    doc_lengths,
    norm_gain,
    router_weight,
    expert_ids,
    gate_quarter,
    up_quarter,
    down_quarter,
):
    vmem = pl.BlockSpec(memory_space=pltpu.VMEM)
    smem = pl.BlockSpec(memory_space=pltpu.SMEM)
    anywhere = pl.BlockSpec(memory_space=pl.ANY)
    dma = pltpu.SemaphoreType.DMA
    hops = NZ // 2
    span = (KS + 1) * T
    return pl.pallas_call(
        kernel,
        out_shape=jax.ShapeDtypeStruct((1, T, D), BF16),
        in_specs=[vmem] * 5 + [smem] + [vmem] * 3 + [anywhere] * 6,
        out_specs=vmem,
        scratch_shapes=[
            pltpu.VMEM((LATENT, HEADS * NOPE), BF16),
            pltpu.VMEM((LATENT, HEADS * NOPE), BF16),
            pltpu.VMEM((HEADS * NOPE, D), BF16),
            pltpu.VMEM((4, D, FQ), BF16),
            pltpu.VMEM((4, D, FQ), BF16),
            pltpu.VMEM((4, FQ, D), BF16),
            pltpu.VMEM((KS + 1, T, LATENT + 2 * ROPE), BF16),
            pltpu.VMEM((span, HEADS * NOPE), BF16),
            pltpu.VMEM((span, HEADS * NOPE), BF16),
            pltpu.VMEM((T, HEADS * NOPE), BF16),
            pltpu.VMEM((T, D), F32),
            pltpu.VMEM((NZ, T, EXTRA + D), BF16),
            pltpu.VMEM((WORK, T), F32),
            pltpu.VMEM((8, WORK), F32),
            pltpu.VMEM((WORK, NZ * T), BF16),
            pltpu.VMEM((NZ * T, WORK), BF16),
            pltpu.VMEM((WORK, D), BF16),
            pltpu.VMEM((WORK, D), BF16),
            pltpu.VMEM((4, WORK, FQ), BF16),
            pltpu.VMEM((WORK, D), BF16),
            pltpu.VMEM((NZ, T, D), BF16),
            pltpu.VMEM((NZ - 1, T, D), BF16),
            dma((6,)),
            dma((KS,)),
            dma((KS,)),
            dma((2, 2)),
            dma((2, 2)),
            dma((2,)),
            dma((2,)),
            dma((2, NJ)),
            dma((2, NJ)),
            dma((NJ,)),
            dma((NJ,)),
            dma((2, hops, NC)),
            dma((2, hops, NC)),
            dma((2 * NY, NC)),
            dma((2 * NY, NC)),
            dma((2 * NY, NJ)),
            dma((2 * NY, NJ)),
            dma((2, hops, NJ)),
            dma((2, hops, NJ)),
        ],
        compiler_params=pltpu.CompilerParams(
            collective_id=0, has_side_effects=True, vmem_limit_bytes=62 * 2**20
        ),
        cost_estimate=pl.CostEstimate(
            flops=24 * 10**9, bytes_accessed=30 * 10**6, transcendentals=10**6
        ),
        name="layer",
    )(
        residual,
        query_nope,
        query_rope,
        latent_rows,
        key_rope,
        doc_lengths,
        norm_gain.reshape(1, D),
        router_weight,
        expert_ids,
        key_up,
        value_up,
        output_proj,
        gate_quarter,
        up_quarter,
        down_quarter,
    )


def solution(mesh):
    in_specs = (
        P("exp", "seq", None),
        P("exp", "seq", None),
        P("exp", "seq", None),
        P("exp", "seq", None),
        P("exp", "seq", None),
        P(),
        P(),
        P(),
        P("exp", None),
        P(),
        P(),
        P("exp", "seq", None),
        P("seq", "exp", None, None),
        P("seq", "exp", None, None),
        P("seq", "exp", None, None),
    )
    return jax.shard_map(
        on_device, mesh=mesh, in_specs=in_specs, out_specs=P("exp", "seq", None), check_vma=False
    )
```

```python
import functools
import math

import jax
import jax.numpy as jnp
from jax import lax
from jax.experimental import pallas as pl
from jax.experimental.pallas import tpu as pltpu
from jax.sharding import PartitionSpec as P

MESH = pl.DeviceIdType.MESH
F32 = jnp.float32
BF16 = jnp.bfloat16

D = 2048
HEADS = 8
NOPE = 128
ROPE = 64
LATENT = 512
TOP = 6
KS = 3
T = 128
EXPERTS = 64
FQ = 352
SLOTS = 12
NX, NY, NZ = 4, 4, 8
BLOCK = NZ * SLOTS
WORK = 2 * NY * BLOCK
EXTRA = 128
NC = 4
CW = D // NC
LATE = 0
AHEAD = 3
PACE = 1
PLAN = {("hop", 6): [("near", 0)], ("hop", 8): [("near", 1)], ("hop", 10): [("on", 0)], ("hop", 13): [("near", 2)], ("hop", 15): [("near", 3)], ("quarter", 1): [("far", 0), ("near", 4)], ("quarter", 2): [("far", 1), ("near", 5)], ("quarter", 3): [("far", 2), ("near", 6)], ("answer", 0): [("far", 3), ("near", 7)], ("answer", 1): [("far", 4)], ("answer", 2): [("far", 5)], ("answer", 3): [("far", 6)], ("answer", 4): [("far", 7)]}
HOP_START, HOP_PACE = 3.5, 3.0
NJ = 8
JW = D // NJ


def dot(a, b):
    return jnp.dot(a, b, preferred_element_type=F32)


def dot_t(a, b):
    return lax.dot_general(a, b, (((1,), (1,)), ((), ())), preferred_element_type=F32)


def t_dot(a, b):
    return lax.dot_general(a, b, (((0,), (0,)), ((), ())), preferred_element_type=F32)


def iota(shape, dim):
    return lax.broadcasted_iota(jnp.int32, shape, dim).astype(F32)


def lanes_of(c):
    if c == 0:
        return pl.ds(0, EXTRA + CW)
    return pl.ds(EXTRA + c * CW, CW)


def kernel(
    residual,
    query_nope,
    query_rope,
    latent,
    rope,
    lengths,
    gain,
    router,
    ids,
    key_up_in,
    value_up_in,
    proj_in,
    gate_in,
    up_in,
    down_in,
    out,
    key_up,
    value_up,
    proj,
    w_gate,
    w_up,
    w_down,
    latents,
    keys,
    values,
    head_out,
    hidden,
    tok,
    code_rows,
    code_cols,
    pick,
    put,
    outbox,
    work,
    units,
    inbox,
    zs,
    zr,
    load_sem,
    a_send,
    a_recv,
    w_send,
    w_recv,
    f_send,
    f_recv,
    d_send,
    d_recv,
    e_send,
    e_recv,
    z_send,
    z_recv,
    y_send,
    y_recv,
    r_send,
    r_recv,
    s_send,
    s_recv,
):
    seq = lax.axis_index("seq")
    exp = lax.axis_index("exp")
    my_y, my_x = lax.div(seq, NX), lax.rem(seq, NX)
    my_z, my_c = lax.div(exp, 2), lax.rem(exp, 2)

    def peer(dx=0, dy=0, dz=0, dc=0):
        x = lax.rem(my_x + (dx + NX), NX)
        y = lax.rem(my_y + (dy + NY), NY)
        z = lax.rem(my_z + (dz + NZ), NZ)
        c = lax.rem(my_c + dc, 2)
        return (y * NX + x, z * 2 + c)

    def later(distance):
        return (lax.rem(seq + (distance + NX * NY), NX * NY), exp)

    def send(src, dst, send_sem, recv_sem, device):
        copy = pltpu.make_async_remote_copy(
            src_ref=src,
            dst_ref=dst,
            send_sem=send_sem,
            recv_sem=recv_sem,
            device_id=device,
            device_id_type=MESH,
        )
        copy.start()
        return copy

    started = []

    loads = []
    for i, (src, dst) in enumerate(
        (
            (key_up_in, key_up),
            (value_up_in, value_up),
            (proj_in, proj),
            (gate_in.at[0, 0], w_gate.at[0]),
            (up_in.at[0, 0], w_up.at[0]),
            (down_in.at[0, 0], w_down.at[0]),
        )
    ):
        copy = pltpu.make_async_copy(src, dst, load_sem.at[i])
        copy.start()
        loads.append(copy)

    partners = [later(d) for d in (1, 2, 3, -1, -2, -3)]
    partners += [peer(dx=1), peer(dx=-1), peer(dz=1), peer(dz=-1)]
    partners += [peer(dy=b // 2, dc=b % 2) for b in range(1, 2 * NY)]
    barrier = pltpu.get_barrier_semaphore()
    for device in partners:
        pl.semaphore_signal(barrier, inc=1, device_id=device, device_id_type=MESH)

    twice = (
        lax.rem(lax.broadcasted_iota(jnp.int32, (ROPE, 2 * ROPE), 1), ROPE)
        == lax.broadcasted_iota(jnp.int32, (ROPE, 2 * ROPE), 0)
    ).astype(F32).astype(BF16)
    latents[0, :, :LATENT] = latent[0]
    latents[0, :, LATENT:] = t_dot(rope[0], twice).astype(BF16)

    pl.semaphore_wait(barrier, len(partners))

    arriving = []
    for d in (1, 2, 3):
        copy = send(latents.at[0], latents.at[d], a_send.at[d - 1], a_recv.at[d - 1], later(d))
        arriving.append(copy)
        started.append(copy)

    near = []
    down_near = {}

    def weights_near():
        for i, (src, dst) in enumerate(((gate_in, w_gate), (up_in, w_up))):
            for way, dx in ((0, 1), (1, -1)):
                copy = send(
                    src.at[0, 0], dst.at[1 + way], w_send.at[i, way], w_recv.at[i, way], peer(dx=dx)
                )
                near.append(copy)
                started.append(copy)

    def down_to_neighbours(j):
        lanes = pl.ds(j * JW, JW)
        for way, dx in ((0, 1), (1, -1)):
            copy = send(
                down_in.at[0, 0, :, lanes],
                w_down.at[1 + way, :, lanes],
                d_send.at[way, j],
                d_recv.at[way, j],
                peer(dx=dx),
            )
            down_near[j, way] = copy
            started.append(copy)

    if not LATE:
        weights_near()

    lane_e = iota((T, EXPERTS), 1)
    id_rows = jnp.concatenate([ids[j].astype(F32) for j in range(TOP)] + [jnp.zeros((2, T), F32)], 0)
    id_cols = id_rows.T
    hits = [(id_cols[:, j : j + 1] == lane_e).astype(F32) for j in range(TOP)]
    named = functools.reduce(jnp.add, hits)
    lower = (
        lax.broadcasted_iota(jnp.int32, (T, T), 0) >= lax.broadcasted_iota(jnp.int32, (T, T), 1)
    ).astype(F32).astype(BF16)
    counted = dot(lower, named.astype(BF16))
    ranks = [jnp.sum(hit * counted, axis=1, keepdims=True) - 1.0 for hit in hits]

    def codes(shape, dim):
        row = iota(shape, dim)
        block = jnp.floor((row + 0.5) * (1.0 / BLOCK))
        rest = row - block * BLOCK
        source = jnp.floor((rest + 0.5) * (1.0 / SLOTS))
        rank = rest - source * SLOTS
        dy = jnp.floor((block + 0.5) * 0.5)
        dc = block - dy * 2.0
        y = dy + my_y.astype(F32)
        y = jnp.where(y >= NY, y - NY, y)
        c = dc + my_c.astype(F32)
        c = jnp.where(c >= 2.0, c - 2.0, c)
        expert = y * 16.0 + my_z.astype(F32) * 2.0 + c
        return source * 1024.0 + expert * 16.0 + rank

    code_rows[...] = codes((WORK, T), 0)
    code_cols[...] = codes((8, WORK), 1)

    loads[0].wait()
    loads[1].wait()

    def project(d):
        rows = pl.ds(pl.multiple_of(d * T, T), T)
        block = latents[d, :, :LATENT]
        keys[rows, :] = dot(block, key_up[...]).astype(BF16)
        values[rows, :] = dot(block, value_up[...]).astype(BF16)

    project(0)
    for copy in arriving:
        copy.wait_recv()
    if LATE:
        weights_near()

    def project_step(d, carry):
        project(d)
        return carry

    lax.fori_loop(1, KS + 1, project_step, 0)

    span = (KS + 1) * T
    first = seq * T
    query_where = first + lax.broadcasted_iota(jnp.int32, (T, 1), 0)
    col = lax.broadcasted_iota(jnp.int32, (1, span), 1)
    key_where = first + lax.rem(col, T) - lax.div(col, T) * T
    query_doc = jnp.zeros((T, 1), jnp.int32)
    key_doc = jnp.zeros((1, span), jnp.int32)
    start = jnp.int32(0)
    for n in range(lengths.shape[1]):
        query_doc += (query_where >= start).astype(jnp.int32)
        key_doc += (key_where >= start).astype(jnp.int32)
        start = start + lengths[0, n]
    allowed = (query_doc == key_doc) & (key_where <= query_where) & (key_where >= 0)
    bias = jnp.where(allowed, 0.0, -1e30)
    scale = 1.0 / math.sqrt(NOPE + ROPE)
    half = lax.broadcasted_iota(jnp.int32, (T, 2 * ROPE), 1) < ROPE

    def head_pair(pair, carry):
        pair_lanes = pl.ds(pl.multiple_of(pair * 128, 128), 128)
        q_pair = query_rope[0, :, pair_lanes]
        for odd in range(2):
            lanes = pl.ds(pl.multiple_of((pair * 2 + odd) * NOPE, 128), NOPE)
            q_two = jnp.where(half, q_pair, 0.0) if odd == 0 else jnp.where(half, 0.0, q_pair)
            q = jnp.concatenate([query_nope[0, :, lanes], q_two.astype(BF16)], axis=1)
            rope_keys = latents[:, :, LATENT:].reshape(span, 2 * ROPE)
            k = jnp.concatenate([keys[:, lanes], rope_keys], axis=1)
            scores = dot_t(q, k) * scale + bias
            weights = jnp.exp(scores - jnp.max(scores, axis=1, keepdims=True))
            totals = jnp.sum(weights, axis=1, keepdims=True)
            mixed = dot(weights.astype(BF16), values[:, lanes])
            head_out[:, lanes] = (mixed / totals).astype(BF16)
        return carry

    lax.fori_loop(0, HEADS // 2, head_pair, 0)

    loads[2].wait()

    def project_out(i, squares):
        lanes = pl.ds(pl.multiple_of(i * 512, 512), 512)
        rows = residual[0, :, lanes].astype(F32) + dot(head_out[...], proj[:, lanes])
        hidden[:, lanes] = rows
        return squares + jnp.sum(rows * rows, axis=1, keepdims=True)

    squares = lax.fori_loop(0, D // 512, project_out, jnp.zeros((T, 1), F32))
    inverse = lax.rsqrt(squares * (1.0 / D) + 1e-06)
    normed = (hidden[...] * inverse * gain[...].astype(F32).reshape(1, D)).astype(BF16)
    tok[0, :, EXTRA:] = normed
    chances = jax.nn.sigmoid(dot_t(normed, router[...]))
    chosen = [jnp.sum(hit * chances, axis=1, keepdims=True) for hit in hits]
    norm_by = 2.446 / functools.reduce(jnp.add, chosen)
    lane = iota((T, EXTRA), 1)
    extra = jnp.zeros((T, EXTRA), F32)
    for j in range(TOP):
        extra = jnp.where(lane == j, id_cols[:, j : j + 1], extra)
        extra = jnp.where(lane == 8 + j, ranks[j], extra)
        extra = jnp.where(lane == 16 + j, chosen[j] * norm_by, extra)
    tok[0, :, :EXTRA] = extra.astype(BF16)

    ring = {}

    def ring_send(c, hop):
        for way, dz in ((0, 1), (1, -1)):
            if hop == NZ // 2 and c % 2 != way:
                continue
            src = (hop - 1) if way == 0 else (NZ - hop + 1) % NZ
            dst = hop if way == 0 else NZ - hop
            lanes = lanes_of(c)
            copy = send(
                tok.at[src, :, lanes],
                tok.at[dst, :, lanes],
                z_send.at[way, hop - 1, c],
                z_recv.at[way, hop - 1, c],
                peer(dz=dz),
            )
            ring[c, hop, way] = copy
            started.append(copy)

    def ring_wait(c, hop):
        for way in range(2):
            if (c, hop, way) in ring:
                ring[c, hop, way].wait_recv()

    def build(s):
        x = tok[s, :, :EXTRA].astype(F32)
        source = (s * 1024).astype(F32)
        x_t = x.T
        rows = code_rows[...]
        match = None
        for j in range(TOP):
            code = x_t[j : j + 1, :] * 16.0 + x_t[8 + j : 9 + j, :] + source
            hit = rows == code
            match = hit if match is None else match | hit
        lanes = pl.ds(pl.multiple_of(s * T, T), T)
        pick[:, lanes] = match.astype(F32).astype(BF16)
        cols = code_cols[0:1, :]
        weight = jnp.zeros((T, WORK), F32)
        for j in range(TOP):
            code = x[:, j : j + 1] * 16.0 + x[:, 8 + j : 9 + j] + source
            weight = jnp.where(cols == code, x[:, 16 + j : 17 + j], weight)
        put[lanes, :] = weight.astype(BF16)

    def build_two(first_s, step, count):
        def body(i, carry):
            build(first_s + i * step)
            return carry

        lax.fori_loop(0, count, body, 0)

    handed = {}

    def hand_out(c):
        lanes = pl.ds(c * CW, CW)
        tok_lanes = pl.ds(EXTRA + c * CW, CW)

        def body(i, carry):
            rows = pl.ds(pl.multiple_of(i * (WORK // 2), WORK // 2), WORK // 2)
            block = tok[:, :, tok_lanes].reshape(NZ * T, CW)
            outbox[rows, lanes] = dot(pick[rows, :], block).astype(BF16)
            return carry

        lax.fori_loop(0, 2, body, 0)
        for b in range(1, 2 * NY):
            rows = pl.ds(b * BLOCK, BLOCK)
            copy = send(
                outbox.at[rows, lanes],
                work.at[rows, lanes],
                y_send.at[b, c],
                y_recv.at[b, c],
                peer(dy=b // 2, dc=b % 2),
            )
            handed[c, b] = copy
            started.append(copy)
        work[:BLOCK, lanes] = outbox[:BLOCK, lanes]

    far = []

    def weights_onward():
        for copy in near:
            copy.wait_recv()
        for way, (ref, dx) in enumerate(((w_gate, 1), (w_up, -1))):
            copy = send(
                ref.at[1 + way], ref.at[3], f_send.at[way], f_recv.at[way], peer(dx=dx)
            )
            far.append(copy)
            started.append(copy)

    down_far = {}

    def down_onward(j):
        lanes = pl.ds(j * JW, JW)
        for way in range(2):
            down_near[j, way].wait_recv()
        way, dx = (0, 1) if j % 2 == 0 else (1, -1)
        copy = send(
            w_down.at[1 + way, :, lanes],
            w_down.at[3, :, lanes],
            e_send.at[j],
            e_recv.at[j],
            peer(dx=dx),
        )
        down_far[j] = copy
        started.append(copy)

    def feed(*place):
        for what, j in PLAN.get(place, ()):
            if what == "on":
                weights_onward()
            elif what == "near":
                down_to_neighbours(j)
            else:
                down_onward(j)

    for c in range(AHEAD):
        ring_send(c, 1)
    build_two(0, 1, 1)
    events = sorted((PACE * c + hop, c, hop) for c in range(NC) for hop in range(1, NZ // 2 + 1))
    for index, (_, c, hop) in enumerate(events):
        ring_wait(c, hop)
        if hop < NZ // 2:
            ring_send(c, hop + 1)
        if hop == 1 and c + AHEAD < NC:
            ring_send(c + AHEAD, 1)
        if c == 0:
            if hop < NZ // 2:
                build_two(hop, NZ - 2 * hop, 2)
            else:
                build_two(hop, 1, 1)
        if hop == NZ // 2:
            hand_out(c)
        feed("hop", index)
    for c in range(NC):
        for b in range(1, 2 * NY):
            handed[c, b].wait_recv()

    for copy in loads[3:]:
        copy.wait()
    tile = 256

    def hidden_units(w):
        def body(i, carry):
            rows = pl.ds(pl.multiple_of(i * tile, tile), tile)
            x = work[rows, :]
            g = dot_t(x, w_gate[w])
            units[w, rows, :] = (g * jax.nn.sigmoid(g) * dot_t(x, w_up[w])).astype(BF16)
            return carry

        lax.fori_loop(0, WORK // tile, body, 0)

    for w in range(4):
        if w == 3:
            for copy in far:
                copy.wait_recv()
        hidden_units(w)
        feed("quarter", w)

    for copy in handed.values():
        copy.wait_send()
    back = {}

    def answer(j):
        lanes = pl.ds(j * JW, JW)
        down_far[j].wait_recv()

        def body(i, carry):
            rows = pl.ds(pl.multiple_of(i * tile, tile), tile)
            total = dot(units[0, rows, :], w_down[0, :, lanes])
            for w in range(1, 4):
                total += dot(units[w, rows, :], w_down[w, :, lanes])
            outbox[rows, lanes] = total.astype(BF16)
            return carry

        lax.fori_loop(0, WORK // tile, body, 0)
        for b in range(1, 2 * NY):
            rows = pl.ds(b * BLOCK, BLOCK)
            copy = send(
                outbox.at[rows, lanes],
                inbox.at[rows, lanes],
                r_send.at[b, j],
                r_recv.at[b, j],
                peer(dy=-(b // 2), dc=b % 2),
            )
            back[j, b] = copy
            started.append(copy)
        inbox[:BLOCK, lanes] = outbox[:BLOCK, lanes]

    sums = {}

    def sum_send(j, way, left):
        lanes = pl.ds(j * JW, JW)
        slot = left if way == 0 else NZ - left
        where = NZ // 2 * 2 - 2 if left == NZ // 2 else way * (NZ // 2 - 1) + left - 1
        copy = send(
            zs.at[slot, :, lanes],
            zr.at[where, :, lanes],
            s_send.at[way, left - 1, j],
            s_recv.at[way, left - 1, j],
            peer(dz=-1 if way == 0 else 1),
        )
        sums[j, way, left] = (copy, where)
        started.append(copy)

    def combine(j):
        lanes = pl.ds(j * JW, JW)
        for b in range(1, 2 * NY):
            back[j, b].wait_recv()

        def body(i, carry):
            rows = pl.ds(pl.multiple_of(i * 2 * T, 2 * T), 2 * T)
            total = dot(put[rows, :], inbox[:, lanes]).astype(BF16)
            zs[2 * i, :, lanes] = total[:T]
            zs[2 * i + 1, :, lanes] = total[T:]
            return carry

        lax.fori_loop(0, NZ // 2, body, 0)
        long_way = j % 2
        sum_send(j, long_way, NZ // 2)
        sum_send(j, 1 - long_way, NZ // 2 - 1)

    def reduce_step(j, hop):
        lanes = pl.ds(j * JW, JW)
        long_way = j % 2
        for way, left in ((long_way, NZ // 2 + 1 - hop), (1 - long_way, NZ // 2 - hop)):
            if left < 1:
                continue
            copy, where = sums[j, way, left]
            copy.wait_recv()
            if left > 1:
                slot = left - 1 if way == 0 else NZ - left + 1
                total = zs[slot, :, lanes].astype(F32) + zr[where, :, lanes].astype(F32)
                zs[slot, :, lanes] = total.astype(BF16)
                sum_send(j, way, left - 1)
        if hop == NZ // 2:
            total = hidden[:, lanes] + zs[0, :, lanes].astype(F32)
            for way in range(2):
                total += zr[sums[j, way, 1][1], :, lanes].astype(F32)
            out[0, :, lanes] = total.astype(BF16)

    steps = []
    for j in range(NJ):
        steps.append((3 * j, 0, j, "answer"))
        steps.append((3 * j + 3.5, 0, j, "combine"))
        for hop in range(1, NZ // 2 + 1):
            steps.append((3 * j + HOP_START + HOP_PACE * hop, 1, j, hop))
    for _, _, j, what in sorted(steps, key=lambda step: step[:3]):
        if what == "answer":
            answer(j)
            feed("answer", j)
        elif what == "combine":
            combine(j)
        else:
            reduce_step(j, what)

    for copy in started:
        if not any(copy is other for other in handed.values()):
            copy.wait_send()


def on_device(
    residual,
    query_nope,
    query_rope,
    latent_rows,
    key_rope,
    key_up,
    value_up,
    output_proj,
    doc_lengths,
    norm_gain,
    router_weight,
    expert_ids,
    gate_quarter,
    up_quarter,
    down_quarter,
):
    vmem = pl.BlockSpec(memory_space=pltpu.VMEM)
    smem = pl.BlockSpec(memory_space=pltpu.SMEM)
    anywhere = pl.BlockSpec(memory_space=pl.ANY)
    dma = pltpu.SemaphoreType.DMA
    hops = NZ // 2
    span = (KS + 1) * T
    return pl.pallas_call(
        kernel,
        out_shape=jax.ShapeDtypeStruct((1, T, D), BF16),
        in_specs=[vmem] * 5 + [smem] + [vmem] * 3 + [anywhere] * 6,
        out_specs=vmem,
        scratch_shapes=[
            pltpu.VMEM((LATENT, HEADS * NOPE), BF16),
            pltpu.VMEM((LATENT, HEADS * NOPE), BF16),
            pltpu.VMEM((HEADS * NOPE, D), BF16),
            pltpu.VMEM((4, FQ, D), BF16),
            pltpu.VMEM((4, FQ, D), BF16),
            pltpu.VMEM((4, FQ, D), BF16),
            pltpu.VMEM((KS + 1, T, LATENT + 2 * ROPE), BF16),
            pltpu.VMEM((span, HEADS * NOPE), BF16),
            pltpu.VMEM((span, HEADS * NOPE), BF16),
            pltpu.VMEM((T, HEADS * NOPE), BF16),
            pltpu.VMEM((T, D), F32),
            pltpu.VMEM((NZ, T, EXTRA + D), BF16),
            pltpu.VMEM((WORK, T), F32),
            pltpu.VMEM((8, WORK), F32),
            pltpu.VMEM((WORK, NZ * T), BF16),
            pltpu.VMEM((NZ * T, WORK), BF16),
            pltpu.VMEM((WORK, D), BF16),
            pltpu.VMEM((WORK, D), BF16),
            pltpu.VMEM((4, WORK, FQ), BF16),
            pltpu.VMEM((WORK, D), BF16),
            pltpu.VMEM((NZ, T, D), BF16),
            pltpu.VMEM((NZ - 1, T, D), BF16),
            dma((6,)),
            dma((KS,)),
            dma((KS,)),
            dma((2, 2)),
            dma((2, 2)),
            dma((2,)),
            dma((2,)),
            dma((2, NJ)),
            dma((2, NJ)),
            dma((NJ,)),
            dma((NJ,)),
            dma((2, hops, NC)),
            dma((2, hops, NC)),
            dma((2 * NY, NC)),
            dma((2 * NY, NC)),
            dma((2 * NY, NJ)),
            dma((2 * NY, NJ)),
            dma((2, hops, NJ)),
            dma((2, hops, NJ)),
        ],
        compiler_params=pltpu.CompilerParams(
            collective_id=0, has_side_effects=True, vmem_limit_bytes=62 * 2**20
        ),
        cost_estimate=pl.CostEstimate(
            flops=24 * 10**9, bytes_accessed=30 * 10**6, transcendentals=10**6
        ),
        name="layer",
    )(
        residual,
        query_nope,
        query_rope,
        latent_rows,
        key_rope.transpose(0, 2, 1),
        doc_lengths,
        norm_gain,
        router_weight.T,
        expert_ids.transpose(2, 0, 1),
        key_up,
        value_up,
        output_proj,
        gate_quarter.transpose(0, 1, 3, 2),
        up_quarter.transpose(0, 1, 3, 2),
        down_quarter,
    )


def solution(mesh):
    in_specs = (
        P("exp", "seq", None),
        P("exp", "seq", None),
        P("exp", "seq", None),
        P("exp", "seq", None),
        P("exp", "seq", None),
        P(),
        P(),
        P(),
        P("exp", None),
        P(),
        P(),
        P("exp", "seq", None),
        P("seq", "exp", None, None),
        P("seq", "exp", None, None),
        P("seq", "exp", None, None),
    )
    return jax.shard_map(
        on_device, mesh=mesh, in_specs=in_specs, out_specs=P("exp", "seq", None), check_vma=False
    )
```

```python
import functools
import math

import jax
import jax.numpy as jnp
from jax import lax
from jax.experimental import pallas as pl
from jax.experimental.pallas import tpu as pltpu
from jax.sharding import PartitionSpec as P

MESH = pl.DeviceIdType.MESH
F32 = jnp.float32
BF16 = jnp.bfloat16

D = 2048
HEADS = 8
NOPE = 128
ROPE = 64
LATENT = 512
TOP = 6
KS = 3
T = 128
EXPERTS = 64
FQ = 352
SLOTS = 12
NX, NY, NZ = 4, 4, 8
BLOCK = NZ * SLOTS
WORK = 2 * NY * BLOCK
EXTRA = 128
NC = 4
CW = D // NC
LATE = 1
AHEAD = 3
PACE = 1
PLAN = {("hop", 6): [("near", 0)], ("hop", 8): [("near", 1)], ("hop", 10): [("on", 0)], ("hop", 13): [("near", 2)], ("hop", 15): [("near", 3)], ("quarter", 1): [("far", 0), ("near", 4)], ("quarter", 2): [("far", 1), ("near", 5)], ("quarter", 3): [("far", 2), ("near", 6)], ("answer", 0): [("far", 3), ("near", 7)], ("answer", 1): [("far", 4)], ("answer", 2): [("far", 5)], ("answer", 3): [("far", 6)], ("answer", 4): [("far", 7)]}
HOP_START, HOP_PACE = 3.5, 3.0
NJ = 8
JW = D // NJ


def dot(a, b):
    return jnp.dot(a, b, preferred_element_type=F32)


def dot_t(a, b):
    return lax.dot_general(a, b, (((1,), (1,)), ((), ())), preferred_element_type=F32)


def t_dot(a, b):
    return lax.dot_general(a, b, (((0,), (0,)), ((), ())), preferred_element_type=F32)


def iota(shape, dim):
    return lax.broadcasted_iota(jnp.int32, shape, dim).astype(F32)


def lanes_of(c):
    if c == 0:
        return pl.ds(0, EXTRA + CW)
    return pl.ds(EXTRA + c * CW, CW)


def kernel(
    residual,
    query_nope,
    query_rope,
    latent,
    rope,
    lengths,
    gain,
    router,
    ids,
    key_up_in,
    value_up_in,
    proj_in,
    gate_in,
    up_in,
    down_in,
    out,
    key_up,
    value_up,
    proj,
    w_gate,
    w_up,
    w_down,
    latents,
    keys,
    values,
    head_out,
    hidden,
    tok,
    code_rows,
    code_cols,
    pick,
    put,
    outbox,
    work,
    units,
    inbox,
    zs,
    zr,
    load_sem,
    a_send,
    a_recv,
    w_send,
    w_recv,
    f_send,
    f_recv,
    d_send,
    d_recv,
    e_send,
    e_recv,
    z_send,
    z_recv,
    y_send,
    y_recv,
    r_send,
    r_recv,
    s_send,
    s_recv,
):
    seq = lax.axis_index("seq")
    exp = lax.axis_index("exp")
    my_y, my_x = lax.div(seq, NX), lax.rem(seq, NX)
    my_z, my_c = lax.div(exp, 2), lax.rem(exp, 2)

    def peer(dx=0, dy=0, dz=0, dc=0):
        x = lax.rem(my_x + (dx + NX), NX)
        y = lax.rem(my_y + (dy + NY), NY)
        z = lax.rem(my_z + (dz + NZ), NZ)
        c = lax.rem(my_c + dc, 2)
        return (y * NX + x, z * 2 + c)

    def later(distance):
        return (lax.rem(seq + (distance + NX * NY), NX * NY), exp)

    def send(src, dst, send_sem, recv_sem, device):
        copy = pltpu.make_async_remote_copy(
            src_ref=src,
            dst_ref=dst,
            send_sem=send_sem,
            recv_sem=recv_sem,
            device_id=device,
            device_id_type=MESH,
        )
        copy.start()
        return copy

    started = []

    loads = []
    for i, (src, dst) in enumerate(
        (
            (key_up_in, key_up),
            (value_up_in, value_up),
            (proj_in, proj),
            (gate_in.at[0, 0], w_gate.at[0]),
            (up_in.at[0, 0], w_up.at[0]),
            (down_in.at[0, 0], w_down.at[0]),
        )
    ):
        copy = pltpu.make_async_copy(src, dst, load_sem.at[i])
        copy.start()
        loads.append(copy)

    partners = [later(d) for d in (1, 2, 3, -1, -2, -3)]
    partners += [peer(dx=1), peer(dx=-1), peer(dz=1), peer(dz=-1)]
    partners += [peer(dy=b // 2, dc=b % 2) for b in range(1, 2 * NY)]
    barrier = pltpu.get_barrier_semaphore()
    for device in partners:
        pl.semaphore_signal(barrier, inc=1, device_id=device, device_id_type=MESH)

    twice = (
        lax.rem(lax.broadcasted_iota(jnp.int32, (ROPE, 2 * ROPE), 1), ROPE)
        == lax.broadcasted_iota(jnp.int32, (ROPE, 2 * ROPE), 0)
    ).astype(F32).astype(BF16)
    latents[0, :, :LATENT] = latent[0]
    latents[0, :, LATENT:] = t_dot(rope[0], twice).astype(BF16)

    pl.semaphore_wait(barrier, len(partners))

    arriving = []
    for d in (1, 2, 3):
        copy = send(latents.at[0], latents.at[d], a_send.at[d - 1], a_recv.at[d - 1], later(d))
        arriving.append(copy)
        started.append(copy)

    near = []
    down_near = {}

    def weights_near(i):
        src, dst = ((gate_in, w_gate), (up_in, w_up))[i]
        for way, dx in ((0, 1), (1, -1)):
            copy = send(
                src.at[0, 0], dst.at[1 + way], w_send.at[i, way], w_recv.at[i, way], peer(dx=dx)
            )
            near.append(copy)
            started.append(copy)

    def down_to_neighbours(j):
        lanes = pl.ds(j * JW, JW)
        for way, dx in ((0, 1), (1, -1)):
            copy = send(
                down_in.at[0, 0, :, lanes],
                w_down.at[1 + way, :, lanes],
                d_send.at[way, j],
                d_recv.at[way, j],
                peer(dx=dx),
            )
            down_near[j, way] = copy
            started.append(copy)

    for i in range(2 - LATE):
        weights_near(i)

    lane_e = iota((T, EXPERTS), 1)
    id_rows = jnp.concatenate([ids[j].astype(F32) for j in range(TOP)] + [jnp.zeros((2, T), F32)], 0)
    id_cols = id_rows.T
    hits = [(id_cols[:, j : j + 1] == lane_e).astype(F32) for j in range(TOP)]
    named = functools.reduce(jnp.add, hits)
    lower = (
        lax.broadcasted_iota(jnp.int32, (T, T), 0) >= lax.broadcasted_iota(jnp.int32, (T, T), 1)
    ).astype(F32).astype(BF16)
    counted = dot(lower, named.astype(BF16))
    ranks = [jnp.sum(hit * counted, axis=1, keepdims=True) - 1.0 for hit in hits]

    def codes(shape, dim):
        row = iota(shape, dim)
        block = jnp.floor((row + 0.5) * (1.0 / BLOCK))
        rest = row - block * BLOCK
        source = jnp.floor((rest + 0.5) * (1.0 / SLOTS))
        rank = rest - source * SLOTS
        dy = jnp.floor((block + 0.5) * 0.5)
        dc = block - dy * 2.0
        y = dy + my_y.astype(F32)
        y = jnp.where(y >= NY, y - NY, y)
        c = dc + my_c.astype(F32)
        c = jnp.where(c >= 2.0, c - 2.0, c)
        expert = y * 16.0 + my_z.astype(F32) * 2.0 + c
        return source * 1024.0 + expert * 16.0 + rank

    code_rows[...] = codes((WORK, T), 0)
    code_cols[...] = codes((8, WORK), 1)

    loads[0].wait()
    loads[1].wait()

    def project(d):
        rows = pl.ds(pl.multiple_of(d * T, T), T)
        block = latents[d, :, :LATENT]
        keys[rows, :] = dot(block, key_up[...]).astype(BF16)
        values[rows, :] = dot(block, value_up[...]).astype(BF16)

    project(0)
    span = (KS + 1) * T
    first = seq * T
    query_where = first + lax.broadcasted_iota(jnp.int32, (T, 1), 0)
    col = lax.broadcasted_iota(jnp.int32, (1, span), 1)
    key_where = first + lax.rem(col, T) - lax.div(col, T) * T
    query_doc = jnp.zeros((T, 1), jnp.int32)
    key_doc = jnp.zeros((1, span), jnp.int32)
    start = jnp.int32(0)
    for n in range(lengths.shape[1]):
        query_doc += (query_where >= start).astype(jnp.int32)
        key_doc += (key_where >= start).astype(jnp.int32)
        start = start + lengths[0, n]
    allowed = (query_doc == key_doc) & (key_where <= query_where) & (key_where >= 0)
    bias = jnp.where(allowed, 0.0, -1e30)
    scale = 1.0 / math.sqrt(NOPE + ROPE)
    for d, copy in enumerate(arriving):
        copy.wait_recv()
        project(d + 1)
    for i in range(2 - LATE, 2):
        weights_near(i)
    half = lax.broadcasted_iota(jnp.int32, (T, 2 * ROPE), 1) < ROPE

    def head_pair(pair, carry):
        pair_lanes = pl.ds(pl.multiple_of(pair * 128, 128), 128)
        q_pair = query_rope[0, :, pair_lanes]
        for odd in range(2):
            lanes = pl.ds(pl.multiple_of((pair * 2 + odd) * NOPE, 128), NOPE)
            q_two = jnp.where(half, q_pair, 0.0) if odd == 0 else jnp.where(half, 0.0, q_pair)
            q = jnp.concatenate([query_nope[0, :, lanes], q_two.astype(BF16)], axis=1)
            rope_keys = latents[:, :, LATENT:].reshape(span, 2 * ROPE)
            k = jnp.concatenate([keys[:, lanes], rope_keys], axis=1)
            scores = dot_t(q, k) * scale + bias
            weights = jnp.exp(scores - jnp.max(scores, axis=1, keepdims=True))
            totals = jnp.sum(weights, axis=1, keepdims=True)
            mixed = dot(weights.astype(BF16), values[:, lanes])
            head_out[:, lanes] = (mixed / totals).astype(BF16)
        return carry

    lax.fori_loop(0, HEADS // 2, head_pair, 0)

    loads[2].wait()

    def project_out(i, squares):
        lanes = pl.ds(pl.multiple_of(i * 512, 512), 512)
        rows = residual[0, :, lanes].astype(F32) + dot(head_out[...], proj[:, lanes])
        hidden[:, lanes] = rows
        return squares + jnp.sum(rows * rows, axis=1, keepdims=True)

    squares = lax.fori_loop(0, D // 512, project_out, jnp.zeros((T, 1), F32))
    inverse = lax.rsqrt(squares * (1.0 / D) + 1e-06)
    normed = (hidden[...] * inverse * gain[...].astype(F32).reshape(1, D)).astype(BF16)
    tok[0, :, EXTRA:] = normed
    chances = jax.nn.sigmoid(dot_t(normed, router[...]))
    chosen = [jnp.sum(hit * chances, axis=1, keepdims=True) for hit in hits]
    norm_by = 2.446 / functools.reduce(jnp.add, chosen)
    lane = iota((T, EXTRA), 1)
    extra = jnp.zeros((T, EXTRA), F32)
    for j in range(TOP):
        extra = jnp.where(lane == j, id_cols[:, j : j + 1], extra)
        extra = jnp.where(lane == 8 + j, ranks[j], extra)
        extra = jnp.where(lane == 16 + j, chosen[j] * norm_by, extra)
    tok[0, :, :EXTRA] = extra.astype(BF16)

    ring = {}

    def ring_send(c, hop):
        for way, dz in ((0, 1), (1, -1)):
            if hop == NZ // 2 and c % 2 != way:
                continue
            src = (hop - 1) if way == 0 else (NZ - hop + 1) % NZ
            dst = hop if way == 0 else NZ - hop
            lanes = lanes_of(c)
            copy = send(
                tok.at[src, :, lanes],
                tok.at[dst, :, lanes],
                z_send.at[way, hop - 1, c],
                z_recv.at[way, hop - 1, c],
                peer(dz=dz),
            )
            ring[c, hop, way] = copy
            started.append(copy)

    def ring_wait(c, hop):
        for way in range(2):
            if (c, hop, way) in ring:
                ring[c, hop, way].wait_recv()

    def build(s):
        x = tok[s, :, :EXTRA].astype(F32)
        source = (s * 1024).astype(F32)
        x_t = x.T
        rows = code_rows[...]
        match = None
        for j in range(TOP):
            code = x_t[j : j + 1, :] * 16.0 + x_t[8 + j : 9 + j, :] + source
            hit = rows == code
            match = hit if match is None else match | hit
        lanes = pl.ds(pl.multiple_of(s * T, T), T)
        pick[:, lanes] = match.astype(F32).astype(BF16)
        cols = code_cols[0:1, :]
        weight = jnp.zeros((T, WORK), F32)
        for j in range(TOP):
            code = x[:, j : j + 1] * 16.0 + x[:, 8 + j : 9 + j] + source
            weight = jnp.where(cols == code, x[:, 16 + j : 17 + j], weight)
        put[lanes, :] = weight.astype(BF16)

    def build_two(first_s, step, count):
        def body(i, carry):
            build(first_s + i * step)
            return carry

        lax.fori_loop(0, count, body, 0)

    handed = {}

    def hand_out(c):
        lanes = pl.ds(c * CW, CW)
        tok_lanes = pl.ds(EXTRA + c * CW, CW)

        def body(i, carry):
            rows = pl.ds(pl.multiple_of(i * (WORK // 2), WORK // 2), WORK // 2)
            block = tok[:, :, tok_lanes].reshape(NZ * T, CW)
            outbox[rows, lanes] = dot(pick[rows, :], block).astype(BF16)
            return carry

        lax.fori_loop(0, 2, body, 0)
        for b in range(1, 2 * NY):
            rows = pl.ds(b * BLOCK, BLOCK)
            copy = send(
                outbox.at[rows, lanes],
                work.at[rows, lanes],
                y_send.at[b, c],
                y_recv.at[b, c],
                peer(dy=b // 2, dc=b % 2),
            )
            handed[c, b] = copy
            started.append(copy)
        work[:BLOCK, lanes] = outbox[:BLOCK, lanes]

    far = []

    def weights_onward():
        for copy in near:
            copy.wait_recv()
        for way, (ref, dx) in enumerate(((w_gate, 1), (w_up, -1))):
            copy = send(
                ref.at[1 + way], ref.at[3], f_send.at[way], f_recv.at[way], peer(dx=dx)
            )
            far.append(copy)
            started.append(copy)

    down_far = {}

    def down_onward(j):
        lanes = pl.ds(j * JW, JW)
        for way in range(2):
            down_near[j, way].wait_recv()
        way, dx = (0, 1) if j % 2 == 0 else (1, -1)
        copy = send(
            w_down.at[1 + way, :, lanes],
            w_down.at[3, :, lanes],
            e_send.at[j],
            e_recv.at[j],
            peer(dx=dx),
        )
        down_far[j] = copy
        started.append(copy)

    def feed(*place):
        for what, j in PLAN.get(place, ()):
            if what == "on":
                weights_onward()
            elif what == "near":
                down_to_neighbours(j)
            else:
                down_onward(j)

    for c in range(AHEAD):
        ring_send(c, 1)
    build_two(0, 1, 1)
    events = sorted((PACE * c + hop, c, hop) for c in range(NC) for hop in range(1, NZ // 2 + 1))
    for index, (_, c, hop) in enumerate(events):
        ring_wait(c, hop)
        if hop < NZ // 2:
            ring_send(c, hop + 1)
        if hop == 1 and c + AHEAD < NC:
            ring_send(c + AHEAD, 1)
        if c == 0:
            if hop < NZ // 2:
                build_two(hop, NZ - 2 * hop, 2)
            else:
                build_two(hop, 1, 1)
        if hop == NZ // 2:
            hand_out(c)
        feed("hop", index)
    for c in range(NC):
        for b in range(1, 2 * NY):
            handed[c, b].wait_recv()

    for copy in loads[3:]:
        copy.wait()
    tile = 256

    def hidden_units(w):
        def body(i, carry):
            rows = pl.ds(pl.multiple_of(i * tile, tile), tile)
            x = work[rows, :]
            g = dot_t(x, w_gate[w])
            units[w, rows, :] = (g * jax.nn.sigmoid(g) * dot_t(x, w_up[w])).astype(BF16)
            return carry

        lax.fori_loop(0, WORK // tile, body, 0)

    for w in range(4):
        if w == 3:
            for copy in far:
                copy.wait_recv()
        hidden_units(w)
        feed("quarter", w)

    for copy in handed.values():
        copy.wait_send()
    back = {}

    def answer(j):
        lanes = pl.ds(j * JW, JW)
        down_far[j].wait_recv()

        def body(i, carry):
            rows = pl.ds(pl.multiple_of(i * tile, tile), tile)
            total = dot(units[0, rows, :], w_down[0, :, lanes])
            for w in range(1, 4):
                total += dot(units[w, rows, :], w_down[w, :, lanes])
            outbox[rows, lanes] = total.astype(BF16)
            return carry

        lax.fori_loop(0, WORK // tile, body, 0)
        for b in range(1, 2 * NY):
            rows = pl.ds(b * BLOCK, BLOCK)
            copy = send(
                outbox.at[rows, lanes],
                inbox.at[rows, lanes],
                r_send.at[b, j],
                r_recv.at[b, j],
                peer(dy=-(b // 2), dc=b % 2),
            )
            back[j, b] = copy
            started.append(copy)
        inbox[:BLOCK, lanes] = outbox[:BLOCK, lanes]

    sums = {}

    def sum_send(j, way, left):
        lanes = pl.ds(j * JW, JW)
        slot = left if way == 0 else NZ - left
        where = NZ // 2 * 2 - 2 if left == NZ // 2 else way * (NZ // 2 - 1) + left - 1
        copy = send(
            zs.at[slot, :, lanes],
            zr.at[where, :, lanes],
            s_send.at[way, left - 1, j],
            s_recv.at[way, left - 1, j],
            peer(dz=-1 if way == 0 else 1),
        )
        sums[j, way, left] = (copy, where)
        started.append(copy)

    def combine(j):
        lanes = pl.ds(j * JW, JW)
        for b in range(1, 2 * NY):
            back[j, b].wait_recv()

        def body(i, carry):
            rows = pl.ds(pl.multiple_of(i * 2 * T, 2 * T), 2 * T)
            total = dot(put[rows, :], inbox[:, lanes]).astype(BF16)
            zs[2 * i, :, lanes] = total[:T]
            zs[2 * i + 1, :, lanes] = total[T:]
            return carry

        lax.fori_loop(0, NZ // 2, body, 0)
        long_way = j % 2
        sum_send(j, long_way, NZ // 2)
        sum_send(j, 1 - long_way, NZ // 2 - 1)

    def reduce_step(j, hop):
        lanes = pl.ds(j * JW, JW)
        long_way = j % 2
        for way, left in ((long_way, NZ // 2 + 1 - hop), (1 - long_way, NZ // 2 - hop)):
            if left < 1:
                continue
            copy, where = sums[j, way, left]
            copy.wait_recv()
            if left > 1:
                slot = left - 1 if way == 0 else NZ - left + 1
                total = zs[slot, :, lanes].astype(F32) + zr[where, :, lanes].astype(F32)
                zs[slot, :, lanes] = total.astype(BF16)
                sum_send(j, way, left - 1)
        if hop == NZ // 2:
            total = hidden[:, lanes] + zs[0, :, lanes].astype(F32)
            for way in range(2):
                total += zr[sums[j, way, 1][1], :, lanes].astype(F32)
            out[0, :, lanes] = total.astype(BF16)

    steps = []
    for j in range(NJ):
        steps.append((3 * j, 0, j, "answer"))
        steps.append((3 * j + 3.5, 0, j, "combine"))
        for hop in range(1, NZ // 2 + 1):
            steps.append((3 * j + HOP_START + HOP_PACE * hop, 1, j, hop))
    for _, _, j, what in sorted(steps, key=lambda step: step[:3]):
        if what == "answer":
            answer(j)
            feed("answer", j)
        elif what == "combine":
            combine(j)
        else:
            reduce_step(j, what)

    for copy in started:
        if not any(copy is other for other in handed.values()):
            copy.wait_send()


def on_device(
    residual,
    query_nope,
    query_rope,
    latent_rows,
    key_rope,
    key_up,
    value_up,
    output_proj,
    doc_lengths,
    norm_gain,
    router_weight,
    expert_ids,
    gate_quarter,
    up_quarter,
    down_quarter,
):
    vmem = pl.BlockSpec(memory_space=pltpu.VMEM)
    smem = pl.BlockSpec(memory_space=pltpu.SMEM)
    anywhere = pl.BlockSpec(memory_space=pl.ANY)
    dma = pltpu.SemaphoreType.DMA
    hops = NZ // 2
    span = (KS + 1) * T
    return pl.pallas_call(
        kernel,
        out_shape=jax.ShapeDtypeStruct((1, T, D), BF16),
        in_specs=[vmem] * 5 + [smem] + [vmem] * 3 + [anywhere] * 6,
        out_specs=vmem,
        scratch_shapes=[
            pltpu.VMEM((LATENT, HEADS * NOPE), BF16),
            pltpu.VMEM((LATENT, HEADS * NOPE), BF16),
            pltpu.VMEM((HEADS * NOPE, D), BF16),
            pltpu.VMEM((4, FQ, D), BF16),
            pltpu.VMEM((4, FQ, D), BF16),
            pltpu.VMEM((4, FQ, D), BF16),
            pltpu.VMEM((KS + 1, T, LATENT + 2 * ROPE), BF16),
            pltpu.VMEM((span, HEADS * NOPE), BF16),
            pltpu.VMEM((span, HEADS * NOPE), BF16),
            pltpu.VMEM((T, HEADS * NOPE), BF16),
            pltpu.VMEM((T, D), F32),
            pltpu.VMEM((NZ, T, EXTRA + D), BF16),
            pltpu.VMEM((WORK, T), F32),
            pltpu.VMEM((8, WORK), F32),
            pltpu.VMEM((WORK, NZ * T), BF16),
            pltpu.VMEM((NZ * T, WORK), BF16),
            pltpu.VMEM((WORK, D), BF16),
            pltpu.VMEM((WORK, D), BF16),
            pltpu.VMEM((4, WORK, FQ), BF16),
            pltpu.VMEM((WORK, D), BF16),
            pltpu.VMEM((NZ, T, D), BF16),
            pltpu.VMEM((NZ - 1, T, D), BF16),
            dma((6,)),
            dma((KS,)),
            dma((KS,)),
            dma((2, 2)),
            dma((2, 2)),
            dma((2,)),
            dma((2,)),
            dma((2, NJ)),
            dma((2, NJ)),
            dma((NJ,)),
            dma((NJ,)),
            dma((2, hops, NC)),
            dma((2, hops, NC)),
            dma((2 * NY, NC)),
            dma((2 * NY, NC)),
            dma((2 * NY, NJ)),
            dma((2 * NY, NJ)),
            dma((2, hops, NJ)),
            dma((2, hops, NJ)),
        ],
        compiler_params=pltpu.CompilerParams(
            collective_id=0, has_side_effects=True, vmem_limit_bytes=62 * 2**20
        ),
        cost_estimate=pl.CostEstimate(
            flops=24 * 10**9, bytes_accessed=30 * 10**6, transcendentals=10**6
        ),
        name="layer",
    )(
        residual,
        query_nope,
        query_rope,
        latent_rows,
        key_rope.transpose(0, 2, 1),
        doc_lengths,
        norm_gain,
        router_weight.T,
        expert_ids.transpose(2, 0, 1),
        key_up,
        value_up,
        output_proj,
        gate_quarter.transpose(0, 1, 3, 2),
        up_quarter.transpose(0, 1, 3, 2),
        down_quarter,
    )


def solution(mesh):
    in_specs = (
        P("exp", "seq", None),
        P("exp", "seq", None),
        P("exp", "seq", None),
        P("exp", "seq", None),
        P("exp", "seq", None),
        P(),
        P(),
        P(),
        P("exp", None),
        P(),
        P(),
        P("exp", "seq", None),
        P("seq", "exp", None, None),
        P("seq", "exp", None, None),
        P("seq", "exp", None, None),
    )
    return jax.shard_map(
        on_device, mesh=mesh, in_specs=in_specs, out_specs=P("exp", "seq", None), check_vma=False
    )
```
